32 devices in a mesh: img: 8 (over z, x), ref: 4 (over y, core).
Axes of the slice: x: 2, y: 2, z: 4, core: 2. Of those that a mesh axis runs over, the one named last changes fastest.
Arguments:
- particles: bfloat16 [2048, 4096], P('img'), may hold values from -40 to 40
- projections: bfloat16 [64, 8, 4096], P(('img', 'ref')), may hold values from -6 to 6
- significance: int32 [8, 64], replicated, may hold values from 0 to 1, as said below
- insertion: int32 [64, 8, 2048], P(('img', 'ref')), may hold values from 0 to 4095
Outputs:
- volume: float32 [2, 131072], P(None, ('img', 'ref'))
- log_evidence: float32 [2048], P('img')
The draws below stay inside these ranges and needn't reach their ends.
Inputs may be any that keep to these rules, and one draw needn't show every extreme that they name: `significance`: runs are blocks o * 2 to o * 2 + 1, o counted over img and ref with img slowest. For each particle block and each run at most one block is significant; particle block q has one in run q * 4; in every draw some particle block has one in every run.
All inputs are finite; a program needn't handle non-finite values.
Results may differ from the reference program's by a relative error of at most 0.00064.
Values may be sent and summed in bfloat16 or wider, within the bound.
A program may use at most 128 MiB of HBM per device.

```python
import math
import jax
import jax.numpy as jnp
from jax import lax

SIDE = 64
PIX = 2048
SHIFTS = 5
PART_DEV = 256
BLK = 8
BPD = 2
VOX = 4096
PARTICLES = 2048
NBLK = 64
VOX_ALL = 131072
N_IMG = 8
N_REF = 4


def projection_values(key):
    return jax.random.truncated_normal(jax.random.fold_in(key, 101), -6.0, 6.0, (NBLK, BLK, 2 * PIX), jnp.float32)


def significance_pattern(key):
    owners = N_IMG * N_REF
    base_key = jax.random.fold_in(key, 202)
    key_level, key_roll, key_which, key_full = jax.random.split(base_key, 4)
    level = jax.random.randint(key_level, (N_IMG, 1), 1, 4)
    rolled = jax.random.randint(key_roll, (N_IMG, owners), 0, 4)
    row_ids = jnp.arange(N_IMG)[:, None]
    column_ids = jnp.arange(owners)[None, :]
    full_row = jax.random.randint(key_full, (), 0, N_IMG)
    live_runs = (rolled < level) | (column_ids == row_ids * N_REF) | (row_ids == full_row)
    which_block = jax.random.randint(key_which, (N_IMG, owners), 0, BPD)
    picked = live_runs[:, :, None] & (which_block[:, :, None] == jnp.arange(BPD)[None, None, :])
    return (picked.astype(jnp.int32).reshape(N_IMG, owners * BPD), which_block)


def draw_projections(key, part):
    return projection_values(key).astype(jnp.bfloat16)


def draw_significance(key, part):
    return significance_pattern(key)[0]


def draw_particles(key, part):
    features = 2 * PIX
    noise_key, pick_key, strength_key = jax.random.split(jax.random.fold_in(key, 303), 3)
    noise = jax.random.truncated_normal(noise_key, -6.0, 6.0, (N_IMG, PART_DEV, features), jnp.float32)
    values = projection_values(key)
    pattern, which_block = significance_pattern(key)
    block_rows = jnp.arange(N_IMG)
    forced = which_block[block_rows, block_rows * N_REF]
    blocks = block_rows * N_REF * BPD + forced
    target = values[blocks, 0] + values[blocks, 1]
    picked = jax.random.randint(pick_key, (N_IMG, PART_DEV, 1), 0, 16) == 0
    strength = jax.random.randint(strength_key, (N_IMG, PART_DEV, 1), 2, 6).astype(jnp.float32)
    amplitude = 25.0 * strength / math.sqrt(features)
    aligned = jnp.clip(amplitude * target[:, None, :] + 0.1 * noise, -40.0, 40.0)
    images = jnp.where(picked, aligned, noise)
    return images.reshape(PARTICLES, features).astype(jnp.bfloat16)


def set_ends(entries, key, smallest, largest):
    extent = entries.shape
    place = [jax.random.randint(jax.random.fold_in(key, axis), (), 0, extent[axis]) for axis in range(len(extent))]
    entries = entries.at[tuple(place)].set(smallest)
    longest = extent.index(max(extent))
    place[longest] = (place[longest] + 1) % extent[longest]
    return entries.at[tuple(place)].set(largest)


def setup_inputs(seed: int = 0) -> dict:
    splits = jax.random.split(jax.random.key(seed), 5)
    return {
        "particles": draw_particles(jax.random.fold_in(splits[4], 71), 0),
        "projections": draw_projections(jax.random.fold_in(splits[4], 71), 0),
        "significance": draw_significance(jax.random.fold_in(splits[4], 71), 0),
        "insertion": set_ends(jax.random.randint(splits[3], (NBLK, BLK, PIX), 0, VOX), jax.random.fold_in(splits[3], 1), 0, VOX - 1).astype(jnp.int32),
    }


SHIFT_X = (0.0, 1.0, -1.0, 0.0, 0.0)
SHIFT_Y = (0.0, 0.0, 0.0, 1.0, -1.0)
NEGATIVE = -1e+30

def shifted_images(images, side_cells):
    pixels = images.shape[1] // 2
    positions = jnp.arange(pixels, dtype=jnp.int32)
    freq_x = (positions % side_cells - side_cells // 2).astype(jnp.float32)
    freq_y = (positions // side_cells).astype(jnp.float32)
    shift_x = jnp.array(SHIFT_X, jnp.float32)[:, None]
    shift_y = jnp.array(SHIFT_Y, jnp.float32)[:, None]
    angles = 2.0 * math.pi / side_cells * (shift_x * freq_x[None, :] + shift_y * freq_y[None, :])
    cosine = jnp.cos(angles)
    sine_table = jnp.sin(angles)
    real_part = images[:, None, :pixels].astype(jnp.float32)
    imag_part = images[:, None, pixels:].astype(jnp.float32)
    new_real = real_part * cosine - imag_part * sine_table
    new_imag = real_part * sine_table + imag_part * cosine
    stacked = jnp.concatenate([new_real, new_imag], axis=2).astype(jnp.bfloat16)
    return stacked.reshape(images.shape[0] * len(SHIFT_X), 2 * pixels)

def reference(particles, projections, significance, insertion):
    owners = N_IMG * N_REF
    features = 2 * PIX
    pattern = significance.reshape(N_IMG, owners, BPD)
    live_blocks = lax.optimization_barrier(jnp.sum(pattern, axis=2))
    chosen = lax.optimization_barrier(jnp.sum(pattern * jnp.arange(BPD, dtype=jnp.int32)[None, None, :], axis=2)).astype(jnp.int32)
    scale_factor = 2.0 / math.sqrt(features)
    images = particles.reshape(N_IMG, PART_DEV, features)

    def one_block(totals, inputs):
        block_images, block_live, block_chosen = inputs
        shifted = shifted_images(block_images, SIDE)
        rows_used = (jnp.arange(owners, dtype=jnp.int32) * BPD + block_chosen).astype(jnp.int32)
        selected = projections[rows_used].reshape(owners * BLK, features)
        scores = jnp.dot(shifted, selected.T, preferred_element_type=jnp.float32) * scale_factor
        scores = scores.reshape(PART_DEV, SHIFTS, owners, BLK)
        valid_mask = jnp.broadcast_to((block_live > 0)[None, None, :, None], scores.shape)
        row_top = lax.optimization_barrier(jnp.max(jnp.where(valid_mask, scores, NEGATIVE), axis=(1, 2, 3)))
        row_total = lax.optimization_barrier(jnp.sum(jnp.where(valid_mask, jnp.exp(scores - row_top[:, None, None, None]), 0.0), axis=(1, 2, 3)))
        evidence = row_top + jnp.log(row_total)
        weights = jnp.where(valid_mask, jnp.exp(scores - evidence[:, None, None, None]), 0.0).astype(jnp.bfloat16)
        weights = weights.reshape(PART_DEV * SHIFTS, owners * BLK)
        partial_value = jnp.dot(weights.T, shifted, preferred_element_type=jnp.float32)
        totals = totals.at[rows_used].add(partial_value.reshape(owners, BLK, features))
        return (totals, evidence)
    initial = jnp.zeros((NBLK, BLK, features), jnp.float32)
    weighted, evidence = lax.scan(one_block, initial, (images, live_blocks, chosen))
    owner_of = (jnp.arange(NBLK, dtype=jnp.int32) // BPD).astype(jnp.int32)
    voxel_ids = (insertion + owner_of[:, None, None] * VOX).reshape(-1)
    real_sum = jax.ops.segment_sum(weighted[:, :, :PIX].reshape(-1), voxel_ids, num_segments=VOX_ALL)
    imag_sum = jax.ops.segment_sum(weighted[:, :, PIX:].reshape(-1), voxel_ids, num_segments=VOX_ALL)
    volume = jnp.stack([real_sum, imag_sum])
    return (volume, evidence.reshape(PARTICLES))
```

```python
import math

import jax
import jax.numpy as jnp
import numpy as np
from jax import lax
from jax.experimental import pallas as pl
from jax.experimental.pallas import tpu as pltpu
from jax.sharding import PartitionSpec as P

SIDE = 64
VOX = 4096
LOW = 128
SHIFTS = 5
NEGATIVE = -1e30
ROWS = 16
COLS = 512
VMEM_BYTES = 56 * 1024 * 1024
NT = (((1,), (1,)), ((), ()))
NN = (((1,), (0,)), ((), ()))


def rotation_tables(pixels):
    positions = np.arange(pixels, dtype=np.int64)
    step = np.float32(2.0 * math.pi / SIDE)
    angle_x = (step * (positions % SIDE - SIDE // 2).astype(np.float32)).astype(np.float64)
    angle_y = (step * (positions // SIDE).astype(np.float32)).astype(np.float64)
    table = np.stack([np.cos(angle_x), np.sin(angle_x), np.cos(angle_y), np.sin(angle_y)])
    return np.concatenate([table, np.zeros_like(table)]).astype(np.float32)


def shift_images(part_ref, table_ref, sh_ref):
    particles, features = part_ref.shape
    pixels = features // 2

    @pl.loop(0, particles // ROWS)
    def _(step):
        rows = pl.ds(pl.multiple_of(step * ROWS, ROWS), ROWS)
        for start in range(0, pixels, COLS):
            left = pl.ds(start, COLS)
            right = pl.ds(pixels + start, COLS)
            real16 = part_ref[rows, left]
            imag16 = part_ref[rows, right]
            sh_ref[0, rows, left] = real16
            sh_ref[0, rows, right] = imag16
            real = real16.astype(jnp.float32)
            imag = imag16.astype(jnp.float32)
            for axis in range(2):
                cosine = table_ref[2 * axis : 2 * axis + 1, left]
                sine = table_ref[2 * axis + 1 : 2 * axis + 2, left]
                real_cos, imag_sin = real * cosine, imag * sine
                real_sin, imag_cos = real * sine, imag * cosine
                plus, minus = 1 + 2 * axis, 2 + 2 * axis
                sh_ref[plus, rows, left] = (real_cos - imag_sin).astype(jnp.bfloat16)
                sh_ref[plus, rows, right] = (real_sin + imag_cos).astype(jnp.bfloat16)
                sh_ref[minus, rows, left] = (real_cos + imag_sin).astype(jnp.bfloat16)
                sh_ref[minus, rows, right] = (imag_cos - real_sin).astype(jnp.bfloat16)


def score_images(sh_ref, arrived, live, score_ref):
    scale = 2.0 / math.sqrt(arrived.shape[1])
    top = None
    for t in range(SHIFTS):
        score = scale * lax.dot_general(arrived, sh_ref[t], NT, preferred_element_type=jnp.float32)
        score = jnp.where(live > 0, score, NEGATIVE)
        score_ref[t] = score
        best = jnp.max(score, axis=0, keepdims=True)
        top = best if top is None else jnp.maximum(top, best)
    total = jnp.zeros_like(top)
    for t in range(SHIFTS):
        terms = jnp.where(live > 0, jnp.exp(score_ref[t] - top), 0.0)
        total = total + jnp.sum(terms, axis=0, keepdims=True)
    return top, total


def merge_stats(tops, totals):
    top = tops[0]
    for other in tops[1:]:
        top = jnp.maximum(top, other)
    total = sum(t * jnp.exp(m - top) for m, t in zip(tops, totals))
    return top + jnp.log(total)


def weigh(score_ref, live, evidence):
    return [
        jnp.where(live > 0, jnp.exp(score_ref[t] - evidence), 0.0).astype(jnp.bfloat16)
        for t in range(SHIFTS)
    ]


def insert_row(ids, real, imag):
    count = ids.shape[1]
    highs = VOX // LOW
    high = jnp.right_shift(ids, 7)
    low = jnp.bitwise_and(ids, LOW - 1)
    hit = lax.broadcasted_iota(jnp.int32, (highs, count), 0) == high
    pieces = []
    for value in (real, imag):
        coarse = value.astype(jnp.bfloat16).astype(jnp.float32)
        for piece in (coarse, value - coarse):
            pieces.append(jnp.where(hit, piece, 0.0).astype(jnp.bfloat16))
    table = lax.broadcasted_iota(jnp.int32, (LOW, count), 0) == low
    table = jnp.where(table, 1.0, 0.0).astype(jnp.bfloat16)
    return lax.dot_general(
        jnp.concatenate(pieces, axis=0), table, NT, preferred_element_type=jnp.float32
    )


def score_kernel(part_ref, table_ref, arrived_ref, live_ref, sh_ref, score_ref, stat_ref):
    shift_images(part_ref, table_ref, sh_ref)
    top, total = score_images(sh_ref, arrived_ref[...], live_ref[...], score_ref)
    stat_ref[0:1, :] = top
    stat_ref[1:2, :] = total


def weight_kernel(sh_ref, score_ref, stat_ref, live_ref, partial_ref, evidence_ref):
    count = stat_ref.shape[0]
    evidence = merge_stats(
        [stat_ref[r, 0:1, :] for r in range(count)], [stat_ref[r, 1:2, :] for r in range(count)]
    )
    evidence_ref[...] = evidence
    weights = weigh(score_ref, live_ref[...], evidence)
    features = sh_ref.shape[2]
    for start in range(0, features, 1024):
        columns = pl.ds(start, 1024)
        partial = None
        for t in range(SHIFTS):
            term = lax.dot_general(
                weights[t], sh_ref[t, :, columns], NN, preferred_element_type=jnp.float32
            )
            partial = term if partial is None else partial + term
        partial_ref[:, columns] = partial


def insert_kernel(returned_ref, request_ref, insertion_ref, volume_ref, weighted_ref):
    img_count, block_rows, features = returned_ref.shape
    blocks = insertion_ref.shape[0]
    pixels = features // 2
    highs = VOX // LOW
    for k in range(blocks):

        def add(q, total):
            return total + jnp.where(request_ref[q, k] > 0, returned_ref[q], 0.0)

        weighted_ref[...] = lax.fori_loop(
            0, img_count, add, jnp.zeros((block_rows, features), jnp.float32)
        )
        slab = jnp.zeros((4 * highs, LOW), jnp.float32)
        for e in range(block_rows):
            slab = slab + insert_row(
                insertion_ref[k, e : e + 1, :],
                weighted_ref[e : e + 1, 0:pixels],
                weighted_ref[e : e + 1, pixels:features],
            )
        for c in range(2):
            part = slab[2 * c * highs : (2 * c + 1) * highs]
            part = part + slab[(2 * c + 1) * highs : (2 * c + 2) * highs]
            volume_ref[c] = part if k == 0 else volume_ref[c] + part


VMEM = pl.BlockSpec(memory_space=pltpu.VMEM)
SMEM = pl.BlockSpec(memory_space=pltpu.SMEM)
PARAMS = pltpu.CompilerParams(vmem_limit_bytes=VMEM_BYTES)


def per_device(particles, projections, significance, insertion):
    img_count = lax.axis_size("img")
    ref_count = lax.axis_size("ref")
    img_rank = lax.axis_index("img")
    ref_rank = lax.axis_index("ref")
    blocks_here, block_rows, features = projections.shape
    particle_count = particles.shape[0]
    width = img_count * block_rows
    pattern = significance.reshape(img_count, img_count, ref_count, blocks_here)
    pattern_ref = lax.dynamic_index_in_dim(pattern, ref_rank, 2, keepdims=False)
    wanted = lax.dynamic_index_in_dim(pattern_ref, img_rank, 0, keepdims=False)
    requested = lax.dynamic_index_in_dim(pattern_ref, img_rank, 1, keepdims=False)
    live = jnp.repeat(jnp.sum(wanted, axis=1), block_rows)[:, None]
    outgoing = jnp.zeros((img_count, block_rows, features), jnp.bfloat16)
    for k in range(blocks_here):
        outgoing = jnp.where(requested[:, k][:, None, None] > 0, projections[k][None], outgoing)
    arrived = lax.all_to_all(outgoing, "img", split_axis=0, concat_axis=0, tiled=True)
    table = jnp.asarray(rotation_tables(features // 2))
    shifted, scores, stats = pl.pallas_call(
        score_kernel,
        out_shape=(
            jax.ShapeDtypeStruct((SHIFTS, particle_count, features), jnp.bfloat16),
            jax.ShapeDtypeStruct((SHIFTS, width, particle_count), jnp.float32),
            jax.ShapeDtypeStruct((2, particle_count), jnp.float32),
        ),
        in_specs=[VMEM] * 4,
        out_specs=(VMEM,) * 3,
        compiler_params=PARAMS,
    )(particles, table, arrived.reshape(width, features), live)
    gathered = lax.all_gather(stats, "ref")
    partial, evidence = pl.pallas_call(
        weight_kernel,
        out_shape=(
            jax.ShapeDtypeStruct((width, features), jnp.float32),
            jax.ShapeDtypeStruct((1, particle_count), jnp.float32),
        ),
        in_specs=[VMEM] * 4,
        out_specs=(VMEM,) * 2,
        compiler_params=PARAMS,
    )(shifted, scores, gathered, live)
    returned = lax.all_to_all(
        partial.reshape(img_count, block_rows, features), "img", split_axis=0, concat_axis=0, tiled=True
    )
    volume = pl.pallas_call(
        insert_kernel,
        out_shape=jax.ShapeDtypeStruct((2, VOX // LOW, LOW), jnp.float32),
        in_specs=[VMEM, SMEM, VMEM],
        out_specs=VMEM,
        scratch_shapes=[pltpu.VMEM((block_rows, features), jnp.float32)],
        compiler_params=PARAMS,
    )(returned, requested, insertion)
    return volume.reshape(2, VOX), evidence.reshape(particle_count)


def solution(mesh):
    in_specs = (P("img", None), P(("img", "ref"), None, None), P(), P(("img", "ref"), None, None))
    out_specs = (P(None, ("img", "ref")), P("img"))
    return jax.shard_map(
        per_device, mesh=mesh, in_specs=in_specs, out_specs=out_specs, check_vma=False
    )
```

```python
import functools
import math

import jax
import jax.numpy as jnp
import numpy as np
from jax import lax
from jax.experimental import pallas as pl
from jax.experimental.pallas import tpu as pltpu
from jax.sharding import PartitionSpec as P

SIDE = 64
VOX = 4096
LOW = 128
SHIFTS = 5
NEGATIVE = -1e30
ROWS = 16
COLS = 512
VMEM_BYTES = 56 * 1024 * 1024
NT = (((1,), (1,)), ((), ()))
NN = (((1,), (0,)), ((), ()))


def rotation_tables(pixels):
    positions = np.arange(pixels, dtype=np.int64)
    step = np.float32(2.0 * math.pi / SIDE)
    angle_x = (step * (positions % SIDE - SIDE // 2).astype(np.float32)).astype(np.float64)
    angle_y = (step * (positions // SIDE).astype(np.float32)).astype(np.float64)
    table = np.stack([np.cos(angle_x), np.sin(angle_x), np.cos(angle_y), np.sin(angle_y)])
    return np.concatenate([table, np.zeros_like(table)]).astype(np.float32)


def shift_images(part_ref, table_ref, sh_ref):
    particles, features = part_ref.shape
    pixels = features // 2

    @pl.loop(0, particles // ROWS)
    def _(step):
        rows = pl.ds(pl.multiple_of(step * ROWS, ROWS), ROWS)
        for start in range(0, pixels, COLS):
            left = pl.ds(start, COLS)
            right = pl.ds(pixels + start, COLS)
            real16 = part_ref[rows, left]
            imag16 = part_ref[rows, right]
            sh_ref[0, rows, left] = real16
            sh_ref[0, rows, right] = imag16
            real = real16.astype(jnp.float32)
            imag = imag16.astype(jnp.float32)
            for axis in range(2):
                cosine = table_ref[2 * axis : 2 * axis + 1, left]
                sine = table_ref[2 * axis + 1 : 2 * axis + 2, left]
                real_cos, imag_sin = real * cosine, imag * sine
                real_sin, imag_cos = real * sine, imag * cosine
                plus, minus = 1 + 2 * axis, 2 + 2 * axis
                sh_ref[plus, rows, left] = (real_cos - imag_sin).astype(jnp.bfloat16)
                sh_ref[plus, rows, right] = (real_sin + imag_cos).astype(jnp.bfloat16)
                sh_ref[minus, rows, left] = (real_cos + imag_sin).astype(jnp.bfloat16)
                sh_ref[minus, rows, right] = (imag_cos - real_sin).astype(jnp.bfloat16)


def score_images(sh_ref, arrived, live, score_ref):
    scale = 2.0 / math.sqrt(arrived.shape[1])
    top = None
    for t in range(SHIFTS):
        score = scale * lax.dot_general(arrived, sh_ref[t], NT, preferred_element_type=jnp.float32)
        score = jnp.where(live > 0, score, NEGATIVE)
        score_ref[t] = score
        best = jnp.max(score, axis=0, keepdims=True)
        top = best if top is None else jnp.maximum(top, best)
    total = jnp.zeros_like(top)
    for t in range(SHIFTS):
        terms = jnp.where(live > 0, jnp.exp(score_ref[t] - top), 0.0)
        total = total + jnp.sum(terms, axis=0, keepdims=True)
    return top, total


def merge_stats(tops, totals):
    top = tops[0]
    for other in tops[1:]:
        top = jnp.maximum(top, other)
    total = sum(t * jnp.exp(m - top) for m, t in zip(tops, totals))
    return top + jnp.log(total)


def weigh(score_ref, live, evidence):
    return [
        jnp.where(live > 0, jnp.exp(score_ref[t] - evidence), 0.0).astype(jnp.bfloat16)
        for t in range(SHIFTS)
    ]


def insert_row(ids, real, imag):
    count = ids.shape[1]
    highs = VOX // LOW
    high = jnp.right_shift(ids, 7)
    low = jnp.bitwise_and(ids, LOW - 1)
    hit = lax.broadcasted_iota(jnp.int32, (highs, count), 0) == high
    pieces = []
    for value in (real, imag):
        coarse = value.astype(jnp.bfloat16).astype(jnp.float32)
        for piece in (coarse, value - coarse):
            pieces.append(jnp.where(hit, piece, 0.0).astype(jnp.bfloat16))
    table = lax.broadcasted_iota(jnp.int32, (LOW, count), 0) == low
    table = jnp.where(table, 1.0, 0.0).astype(jnp.bfloat16)
    return lax.dot_general(
        jnp.concatenate(pieces, axis=0), table, NT, preferred_element_type=jnp.float32
    )


MESH = pl.DeviceIdType.MESH


def step_kernel(
    img_count,
    ref_count,
    sig_ref,
    part_ref,
    table_ref,
    proj_ref,
    ids_ref,
    volume_ref,
    evidence_ref,
    sh_ref,
    out_ref,
    slot_ref,
    arrived_ref,
    live_ref,
    score_ref,
    stat_ref,
    partial_ref,
    return_ref,
    block_send,
    block_recv,
    stat_send,
    stat_recv,
    sum_send,
    sum_recv,
):
    img = lax.axis_index("img")
    ref = lax.axis_index("ref")
    blocks, block_rows, features = proj_ref.shape
    pixels = features // 2
    chunks, _, _, span = partial_ref.shape
    half = span // 2
    particles = part_ref.shape[0]

    barrier = pltpu.get_barrier_semaphore()
    for d in range(1, img_count):
        pl.semaphore_signal(
            barrier, inc=1, device_id={"img": lax.rem(img + d, img_count)}, device_id_type=MESH
        )
    for d in range(1, ref_count):
        pl.semaphore_signal(
            barrier, inc=1, device_id={"ref": lax.rem(ref + d, ref_count)}, device_id_type=MESH
        )

    own = (img * ref_count + ref) * blocks

    def asked(d, k):
        return sig_ref[lax.rem(img + d, img_count), own + k]

    for d in range(img_count):
        chosen = jnp.zeros((block_rows, features), jnp.float32)
        for k in range(blocks):
            chosen = jnp.where(asked(d, k) > 0, proj_ref[k].astype(jnp.float32), chosen)
        chosen = jnp.concatenate([chosen[:, :pixels], chosen[:, pixels:]], axis=0)
        out_ref[d] = chosen.astype(jnp.bfloat16)
    pl.semaphore_wait(barrier, img_count + ref_count - 2)

    block_copies = {}
    for d in range(1, img_count):
        block_copies[d] = pltpu.make_async_remote_copy(
            src_ref=out_ref.at[d],
            dst_ref=slot_ref.at[d],
            send_sem=block_send.at[d],
            recv_sem=block_recv.at[d],
            device_id={"img": lax.rem(img + d, img_count)},
            device_id_type=MESH,
        )
        block_copies[d].start()

    for d in range(img_count):
        alive = jnp.int32(0)
        source = lax.rem(img - d + img_count, img_count)
        for k in range(blocks):
            alive = alive + sig_ref[img, (source * ref_count + ref) * blocks + k]
        live_ref[pl.ds(d * block_rows, block_rows), :] = jnp.full(
            (block_rows, particles), alive.astype(jnp.float32)
        )
    shift_images(part_ref, table_ref, sh_ref)

    slot_ref[0] = out_ref[0]
    for d in range(1, img_count):
        block_copies[d].wait_recv()
    for d in range(0, img_count, 2):
        pair = [slot_ref[d].astype(jnp.float32), slot_ref[d + 1].astype(jnp.float32)]
        for c in range(2):
            rows = jnp.concatenate([p[c * block_rows : (c + 1) * block_rows] for p in pair], axis=0)
            arrived_ref[pl.ds(d * block_rows, 2 * block_rows), pl.ds(c * pixels, pixels)] = rows.astype(
                jnp.bfloat16
            )

    live = live_ref[...]
    top, total = score_images(sh_ref, arrived_ref[...], live, score_ref)
    stat_ref[0] = jnp.zeros_like(stat_ref[0])
    stat_ref[0, 0:1, :] = top
    stat_ref[0, 1:2, :] = total
    stat_copies = []
    for d in range(1, ref_count):
        copy = pltpu.make_async_remote_copy(
            src_ref=stat_ref.at[0],
            dst_ref=stat_ref.at[d],
            send_sem=stat_send.at[d],
            recv_sem=stat_recv.at[d],
            device_id={"ref": lax.rem(ref + d, ref_count)},
            device_id_type=MESH,
        )
        copy.start()
        stat_copies.append(copy)
    for copy in stat_copies:
        copy.wait_recv()
    evidence = merge_stats(
        [stat_ref[r, 0:1, :] for r in range(ref_count)],
        [stat_ref[r, 1:2, :] for r in range(ref_count)],
    )
    evidence_ref[...] = evidence
    weights = weigh(score_ref, live, evidence)

    sum_copies = [[] for _ in range(chunks)]
    for j in range(chunks):
        for c in range(2):
            columns = pl.ds(c * pixels + j * half, half)
            partial = None
            for t in range(SHIFTS):
                term = lax.dot_general(
                    weights[t], sh_ref[t, :, columns], NN, preferred_element_type=jnp.float32
                )
                partial = term if partial is None else partial + term
            for d in range(img_count):
                rows = partial[d * block_rows : (d + 1) * block_rows]
                partial_ref[j, d, :, pl.ds(c * half, half)] = rows
        for d in range(1, img_count):
            copy = pltpu.make_async_remote_copy(
                src_ref=partial_ref.at[j, d],
                dst_ref=return_ref.at[j, d],
                send_sem=sum_send.at[j, d],
                recv_sem=sum_recv.at[j, d],
                device_id={"img": lax.rem(img - d + img_count, img_count)},
                device_id_type=MESH,
            )
            copy.start()
            sum_copies[j].append(copy)

    highs = VOX // LOW
    slab = jnp.zeros((4 * highs, LOW), jnp.float32)
    for j in range(chunks):
        for copy in sum_copies[j]:
            copy.wait_recv()
        for k in range(blocks):
            weighted = jnp.where(asked(0, k) > 0, partial_ref[j, 0], 0.0)
            for d in range(1, img_count):
                weighted = weighted + jnp.where(asked(d, k) > 0, return_ref[j, d], 0.0)
            for e in range(block_rows):
                slab = slab + insert_row(
                    ids_ref[k, e : e + 1, pl.ds(j * half, half)],
                    weighted[e : e + 1, :half],
                    weighted[e : e + 1, half:],
                )
    for c in range(2):
        part = slab[2 * c * highs : (2 * c + 1) * highs]
        volume_ref[c] = part + slab[(2 * c + 1) * highs : (2 * c + 2) * highs]

    for d in range(1, img_count):
        block_copies[d].wait_send()
    for copy in stat_copies:
        copy.wait_send()
    for copies in sum_copies:
        for copy in copies:
            copy.wait_send()


VMEM = pl.BlockSpec(memory_space=pltpu.VMEM)
SMEM = pl.BlockSpec(memory_space=pltpu.SMEM)
CHUNKS = 4


def per_device(particles, projections, significance, insertion):
    img_count = lax.axis_size("img")
    ref_count = lax.axis_size("ref")
    blocks_here, block_rows, features = projections.shape
    particle_count = particles.shape[0]
    width = img_count * block_rows
    pixels = features // 2
    table = jnp.asarray(rotation_tables(pixels))
    volume, evidence = pl.pallas_call(
        functools.partial(step_kernel, img_count, ref_count),
        out_shape=(
            jax.ShapeDtypeStruct((2, VOX // LOW, LOW), jnp.float32),
            jax.ShapeDtypeStruct((1, particle_count), jnp.float32),
        ),
        in_specs=[SMEM] + [VMEM] * 4,
        out_specs=(VMEM,) * 2,
        scratch_shapes=[
            pltpu.VMEM((SHIFTS, particle_count, features), jnp.bfloat16),
            pltpu.VMEM((img_count, 2 * block_rows, pixels), jnp.bfloat16),
            pltpu.VMEM((img_count, 2 * block_rows, pixels), jnp.bfloat16),
            pltpu.VMEM((width, features), jnp.bfloat16),
            pltpu.VMEM((width, particle_count), jnp.float32),
            pltpu.VMEM((SHIFTS, width, particle_count), jnp.float32),
            pltpu.VMEM((ref_count, 8, particle_count), jnp.float32),
            pltpu.VMEM((CHUNKS, img_count, block_rows, features // CHUNKS), jnp.float32),
            pltpu.VMEM((CHUNKS, img_count, block_rows, features // CHUNKS), jnp.float32),
            pltpu.SemaphoreType.DMA((img_count,)),
            pltpu.SemaphoreType.DMA((img_count,)),
            pltpu.SemaphoreType.DMA((ref_count,)),
            pltpu.SemaphoreType.DMA((ref_count,)),
            pltpu.SemaphoreType.DMA((CHUNKS, img_count)),
            pltpu.SemaphoreType.DMA((CHUNKS, img_count)),
        ],
        compiler_params=pltpu.CompilerParams(
            vmem_limit_bytes=VMEM_BYTES, collective_id=0, has_side_effects=True
        ),
    )(significance, particles, table, projections, insertion)
    return volume.reshape(2, VOX), evidence.reshape(particle_count)


def solution(mesh):
    in_specs = (P("img", None), P(("img", "ref"), None, None), P(), P(("img", "ref"), None, None))
    out_specs = (P(None, ("img", "ref")), P("img"))
    return jax.shard_map(
        per_device, mesh=mesh, in_specs=in_specs, out_specs=out_specs, check_vma=False
    )
```

```python
import functools
import math

import jax
import jax.numpy as jnp
import numpy as np
from jax import lax
from jax.experimental import pallas as pl
from jax.experimental.pallas import tpu as pltpu
from jax.sharding import PartitionSpec as P

SIDE = 64
VOX = 4096
LOW = 128
SHIFTS = 5
NEGATIVE = -1e30
ROWS = 16
COLS = 512
VMEM_BYTES = 56 * 1024 * 1024
NT = (((1,), (1,)), ((), ()))
NN = (((1,), (0,)), ((), ()))


def rotation_tables(pixels):
    positions = np.arange(pixels, dtype=np.int64)
    step = np.float32(2.0 * math.pi / SIDE)
    angle_x = (step * (positions % SIDE - SIDE // 2).astype(np.float32)).astype(np.float64)
    angle_y = (step * (positions // SIDE).astype(np.float32)).astype(np.float64)
    table = np.stack([np.cos(angle_x), np.sin(angle_x), np.cos(angle_y), np.sin(angle_y)])
    return np.concatenate([table, np.zeros_like(table)]).astype(np.float32)


def shift_images(part_ref, table_ref, sh_ref):
    particles, features = part_ref.shape
    pixels = features // 2

    @pl.loop(0, particles // ROWS)
    def _(step):
        rows = pl.ds(pl.multiple_of(step * ROWS, ROWS), ROWS)
        for start in range(0, pixels, COLS):
            left = pl.ds(start, COLS)
            right = pl.ds(pixels + start, COLS)
            real16 = part_ref[rows, left]
            imag16 = part_ref[rows, right]
            sh_ref[0, rows, left] = real16
            sh_ref[0, rows, right] = imag16
            real = real16.astype(jnp.float32)
            imag = imag16.astype(jnp.float32)
            for axis in range(2):
                cosine = table_ref[2 * axis : 2 * axis + 1, left]
                sine = table_ref[2 * axis + 1 : 2 * axis + 2, left]
                real_cos, imag_sin = real * cosine, imag * sine
                real_sin, imag_cos = real * sine, imag * cosine
                plus, minus = 1 + 2 * axis, 2 + 2 * axis
                sh_ref[plus, rows, left] = (real_cos - imag_sin).astype(jnp.bfloat16)
                sh_ref[plus, rows, right] = (real_sin + imag_cos).astype(jnp.bfloat16)
                sh_ref[minus, rows, left] = (real_cos + imag_sin).astype(jnp.bfloat16)
                sh_ref[minus, rows, right] = (imag_cos - real_sin).astype(jnp.bfloat16)


def score_images(sh_ref, arrived, live, score_ref):
    scale = 2.0 / math.sqrt(arrived.shape[1])
    top = None
    for t in range(SHIFTS):
        score = scale * lax.dot_general(arrived, sh_ref[t], NT, preferred_element_type=jnp.float32)
        score = jnp.where(live > 0, score, NEGATIVE)
        score_ref[t] = score
        best = jnp.max(score, axis=0, keepdims=True)
        top = best if top is None else jnp.maximum(top, best)
    total = jnp.zeros_like(top)
    for t in range(SHIFTS):
        terms = jnp.where(live > 0, jnp.exp(score_ref[t] - top), 0.0)
        total = total + jnp.sum(terms, axis=0, keepdims=True)
    return top, total


def merge_stats(tops, totals):
    top = tops[0]
    for other in tops[1:]:
        top = jnp.maximum(top, other)
    total = sum(t * jnp.exp(m - top) for m, t in zip(tops, totals))
    return top + jnp.log(total)


def weigh(score_ref, live, evidence):
    return [
        jnp.where(live > 0, jnp.exp(score_ref[t] - evidence), 0.0).astype(jnp.bfloat16)
        for t in range(SHIFTS)
    ]


def insert_row(ids, real, imag):
    count = ids.shape[1]
    highs = VOX // LOW
    high = jnp.right_shift(ids, 7)
    low = jnp.bitwise_and(ids, LOW - 1)
    hit = lax.broadcasted_iota(jnp.int32, (highs, count), 0) == high
    pieces = []
    for value in (real, imag):
        coarse = value.astype(jnp.bfloat16).astype(jnp.float32)
        for piece in (coarse, value - coarse):
            pieces.append(jnp.where(hit, piece, 0.0).astype(jnp.bfloat16))
    table = lax.broadcasted_iota(jnp.int32, (LOW, count), 0) == low
    table = jnp.where(table, 1.0, 0.0).astype(jnp.bfloat16)
    return lax.dot_general(
        jnp.concatenate(pieces, axis=0), table, NT, preferred_element_type=jnp.float32
    )


MESH = pl.DeviceIdType.MESH


def step_kernel(
    img_count,
    ref_count,
    sig_ref,
    part_ref,
    table_ref,
    proj_ref,
    ids_ref,
    volume_ref,
    evidence_ref,
    sh_ref,
    out_ref,
    slot_ref,
    arrived_ref,
    live_ref,
    score_ref,
    stat_ref,
    partial_ref,
    return_ref,
    far_ref,
    joint_ref,
    joined_ref,
    block_send,
    block_recv,
    stat_send,
    stat_recv,
    sum_send,
    sum_recv,
    far_send,
    far_recv,
    join_send,
    join_recv,
):
    img = lax.axis_index("img")
    ref = lax.axis_index("ref")
    blocks, block_rows, features = proj_ref.shape
    pixels = features // 2
    chunks, _, _, span = partial_ref.shape
    half = span // 2
    particles = part_ref.shape[0]

    side = img_count // 2
    place = lax.rem(img, side)
    base = img - place
    mirror = lax.rem(img + side, img_count)

    def ahead(d):
        return lax.rem(base + (d // side) * side, img_count) + lax.rem(place + d % side, side)

    def behind(d):
        return lax.rem(base + (d // side) * side, img_count) + lax.rem(place - d % side + side, side)

    barrier = pltpu.get_barrier_semaphore()
    for d in range(1, img_count):
        pl.semaphore_signal(barrier, inc=1, device_id={"img": ahead(d)}, device_id_type=MESH)
    for d in range(1, ref_count):
        pl.semaphore_signal(
            barrier, inc=1, device_id={"ref": lax.rem(ref + d, ref_count)}, device_id_type=MESH
        )

    own = (img * ref_count + ref) * blocks

    def asked(d, k):
        return sig_ref[ahead(d), own + k]

    def asked_mirror(d, k):
        return sig_ref[ahead(d), (mirror * ref_count + ref) * blocks + k]

    for d in range(img_count):
        chosen = jnp.zeros((block_rows, features), jnp.float32)
        for k in range(blocks):
            chosen = jnp.where(asked(d, k) > 0, proj_ref[k].astype(jnp.float32), chosen)
        chosen = jnp.concatenate([chosen[:, :pixels], chosen[:, pixels:]], axis=0)
        out_ref[d] = chosen.astype(jnp.bfloat16)
    pl.semaphore_wait(barrier, img_count + ref_count - 2)

    block_copies = {}
    for d in range(1, img_count):
        block_copies[d] = pltpu.make_async_remote_copy(
            src_ref=out_ref.at[d],
            dst_ref=slot_ref.at[d],
            send_sem=block_send.at[d],
            recv_sem=block_recv.at[d],
            device_id={"img": ahead(d)},
            device_id_type=MESH,
        )
        block_copies[d].start()

    for d in range(img_count):
        alive = jnp.int32(0)
        source = behind(d)
        for k in range(blocks):
            alive = alive + sig_ref[img, (source * ref_count + ref) * blocks + k]
        live_ref[pl.ds(d * block_rows, block_rows), :] = jnp.full(
            (block_rows, particles), alive.astype(jnp.float32)
        )
    shift_images(part_ref, table_ref, sh_ref)

    slot_ref[0] = out_ref[0]
    for d in range(1, img_count):
        block_copies[d].wait_recv()
    for d in range(0, img_count, 2):
        pair = [slot_ref[d].astype(jnp.float32), slot_ref[d + 1].astype(jnp.float32)]
        for c in range(2):
            rows = jnp.concatenate([p[c * block_rows : (c + 1) * block_rows] for p in pair], axis=0)
            arrived_ref[pl.ds(d * block_rows, 2 * block_rows), pl.ds(c * pixels, pixels)] = rows.astype(
                jnp.bfloat16
            )

    live = live_ref[...]
    top, total = score_images(sh_ref, arrived_ref[...], live, score_ref)
    stat_ref[0] = jnp.zeros_like(stat_ref[0])
    stat_ref[0, 0:1, :] = top
    stat_ref[0, 1:2, :] = total
    stat_copies = []
    for d in range(1, ref_count):
        copy = pltpu.make_async_remote_copy(
            src_ref=stat_ref.at[0],
            dst_ref=stat_ref.at[d],
            send_sem=stat_send.at[d],
            recv_sem=stat_recv.at[d],
            device_id={"ref": lax.rem(ref + d, ref_count)},
            device_id_type=MESH,
        )
        copy.start()
        stat_copies.append(copy)
    for copy in stat_copies:
        copy.wait_recv()
    evidence = merge_stats(
        [stat_ref[r, 0:1, :] for r in range(ref_count)],
        [stat_ref[r, 1:2, :] for r in range(ref_count)],
    )
    evidence_ref[...] = evidence
    weights = weigh(score_ref, live, evidence)

    sum_copies = [[] for _ in range(chunks)]
    far_copies = [[] for _ in range(chunks)]
    join_copies = []

    def join(j):
        for copy in far_copies[j]:
            copy.wait_recv()
        for k in range(blocks):
            joint = jnp.where(asked_mirror(0, k) > 0, partial_ref[j, side], 0.0)
            for d in range(1, side):
                joint = joint + jnp.where(asked_mirror(d, k) > 0, far_ref[j, d], 0.0)
            joint_ref[j, k] = joint
        copy = pltpu.make_async_remote_copy(
            src_ref=joint_ref.at[j],
            dst_ref=joined_ref.at[j],
            send_sem=join_send.at[j],
            recv_sem=join_recv.at[j],
            device_id={"img": mirror},
            device_id_type=MESH,
        )
        copy.start()
        join_copies.append(copy)

    for j in range(chunks):
        for c in range(2):
            columns = pl.ds(c * pixels + j * half, half)
            partial = None
            for t in range(SHIFTS):
                term = lax.dot_general(
                    weights[t], sh_ref[t, :, columns], NN, preferred_element_type=jnp.float32
                )
                partial = term if partial is None else partial + term
            for d in range(img_count):
                rows = partial[d * block_rows : (d + 1) * block_rows]
                partial_ref[j, d, :, pl.ds(c * half, half)] = rows
        for d in range(1, side):
            copy = pltpu.make_async_remote_copy(
                src_ref=partial_ref.at[j, side + d],
                dst_ref=far_ref.at[j, d],
                send_sem=far_send.at[j, d],
                recv_sem=far_recv.at[j, d],
                device_id={"img": behind(d)},
                device_id_type=MESH,
            )
            copy.start()
            far_copies[j].append(copy)
        for d in range(1, side):
            copy = pltpu.make_async_remote_copy(
                src_ref=partial_ref.at[j, d],
                dst_ref=return_ref.at[j, d],
                send_sem=sum_send.at[j, d],
                recv_sem=sum_recv.at[j, d],
                device_id={"img": behind(d)},
                device_id_type=MESH,
            )
            copy.start()
            sum_copies[j].append(copy)
        if j > 0:
            join(j - 1)
    join(chunks - 1)

    highs = VOX // LOW
    slab = jnp.zeros((4 * highs, LOW), jnp.float32)
    for j in range(chunks):
        for copy in sum_copies[j]:
            copy.wait_recv()
        join_copies[j].wait_recv()
        for k in range(blocks):
            weighted = joined_ref[j, k] + jnp.where(asked(0, k) > 0, partial_ref[j, 0], 0.0)
            for d in range(1, side):
                weighted = weighted + jnp.where(asked(d, k) > 0, return_ref[j, d], 0.0)
            for e in range(block_rows):
                slab = slab + insert_row(
                    ids_ref[k, e : e + 1, pl.ds(j * half, half)],
                    weighted[e : e + 1, :half],
                    weighted[e : e + 1, half:],
                )
    for c in range(2):
        part = slab[2 * c * highs : (2 * c + 1) * highs]
        part = part + slab[(2 * c + 1) * highs : (2 * c + 2) * highs]
        for h in range(highs):
            volume_ref[c : c + 1, h * LOW : (h + 1) * LOW] = part[h : h + 1]

    for d in range(1, img_count):
        block_copies[d].wait_send()
    for copy in stat_copies:
        copy.wait_send()
    for copies in sum_copies + far_copies + [join_copies]:
        for copy in copies:
            copy.wait_send()


VMEM = pl.BlockSpec(memory_space=pltpu.VMEM)
SMEM = pl.BlockSpec(memory_space=pltpu.SMEM)
CHUNKS = 4


def per_device(particles, projections, significance, insertion):
    img_count = lax.axis_size("img")
    ref_count = lax.axis_size("ref")
    blocks_here, block_rows, features = projections.shape
    particle_count = particles.shape[0]
    width = img_count * block_rows
    pixels = features // 2
    table = jnp.asarray(rotation_tables(pixels))
    volume, evidence = pl.pallas_call(
        functools.partial(step_kernel, img_count, ref_count),
        out_shape=(
            jax.ShapeDtypeStruct((2, VOX), jnp.float32),
            jax.ShapeDtypeStruct((1, particle_count), jnp.float32),
        ),
        in_specs=[SMEM] + [VMEM] * 4,
        out_specs=(VMEM,) * 2,
        scratch_shapes=[
            pltpu.VMEM((SHIFTS, particle_count, features), jnp.bfloat16),
            pltpu.VMEM((img_count, 2 * block_rows, pixels), jnp.bfloat16),
            pltpu.VMEM((img_count, 2 * block_rows, pixels), jnp.bfloat16),
            pltpu.VMEM((width, features), jnp.bfloat16),
            pltpu.VMEM((width, particle_count), jnp.float32),
            pltpu.VMEM((SHIFTS, width, particle_count), jnp.float32),
            pltpu.VMEM((ref_count, 8, particle_count), jnp.float32),
            pltpu.VMEM((CHUNKS, img_count, block_rows, features // CHUNKS), jnp.float32),
            pltpu.VMEM((CHUNKS, img_count // 2, block_rows, features // CHUNKS), jnp.float32),
            pltpu.VMEM((CHUNKS, img_count // 2, block_rows, features // CHUNKS), jnp.float32),
            pltpu.VMEM((CHUNKS, blocks_here, block_rows, features // CHUNKS), jnp.float32),
            pltpu.VMEM((CHUNKS, blocks_here, block_rows, features // CHUNKS), jnp.float32),
            pltpu.SemaphoreType.DMA((img_count,)),
            pltpu.SemaphoreType.DMA((img_count,)),
            pltpu.SemaphoreType.DMA((ref_count,)),
            pltpu.SemaphoreType.DMA((ref_count,)),
            pltpu.SemaphoreType.DMA((CHUNKS, img_count // 2)),
            pltpu.SemaphoreType.DMA((CHUNKS, img_count // 2)),
            pltpu.SemaphoreType.DMA((CHUNKS, img_count // 2)),
            pltpu.SemaphoreType.DMA((CHUNKS, img_count // 2)),
            pltpu.SemaphoreType.DMA((CHUNKS,)),
            pltpu.SemaphoreType.DMA((CHUNKS,)),
        ],
        compiler_params=pltpu.CompilerParams(
            vmem_limit_bytes=VMEM_BYTES, collective_id=0, has_side_effects=True
        ),
    )(significance, particles, table, projections, insertion)
    return volume, evidence.reshape(particle_count)


def solution(mesh):
    in_specs = (P("img", None), P(("img", "ref"), None, None), P(), P(("img", "ref"), None, None))
    out_specs = (P(None, ("img", "ref")), P("img"))
    return jax.shard_map(
        per_device, mesh=mesh, in_specs=in_specs, out_specs=out_specs, check_vma=False
    )
```

```python
import functools
import math

import jax
import jax.numpy as jnp
import numpy as np
from jax import lax
from jax.experimental import pallas as pl
from jax.experimental.pallas import tpu as pltpu
from jax.sharding import PartitionSpec as P

SIDE = 64
VOX = 4096
LOW = 128
SHIFTS = 5
NEGATIVE = -1e30
ROWS = 16
COLS = 512
VMEM_BYTES = 56 * 1024 * 1024
NT = (((1,), (1,)), ((), ()))
NN = (((1,), (0,)), ((), ()))


def rotation_tables(pixels):
    positions = np.arange(pixels, dtype=np.int64)
    step = np.float32(2.0 * math.pi / SIDE)
    angle_x = (step * (positions % SIDE - SIDE // 2).astype(np.float32)).astype(np.float64)
    angle_y = (step * (positions // SIDE).astype(np.float32)).astype(np.float64)
    table = np.stack([np.cos(angle_x), np.sin(angle_x), np.cos(angle_y), np.sin(angle_y)])
    return np.concatenate([table, np.zeros_like(table)]).astype(np.float32)


def shift_images(part_ref, table_ref, sh_ref):
    particles, features = part_ref.shape
    pixels = features // 2

    @pl.loop(0, particles // ROWS)
    def _(step):
        rows = pl.ds(pl.multiple_of(step * ROWS, ROWS), ROWS)
        for start in range(0, pixels, COLS):
            left = pl.ds(start, COLS)
            right = pl.ds(pixels + start, COLS)
            real16 = part_ref[rows, left]
            imag16 = part_ref[rows, right]
            sh_ref[0, rows, left] = real16
            sh_ref[0, rows, right] = imag16
            real = real16.astype(jnp.float32)
            imag = imag16.astype(jnp.float32)
            for axis in range(2):
                cosine = table_ref[2 * axis : 2 * axis + 1, left]
                sine = table_ref[2 * axis + 1 : 2 * axis + 2, left]
                real_cos, imag_sin = real * cosine, imag * sine
                real_sin, imag_cos = real * sine, imag * cosine
                plus, minus = 1 + 2 * axis, 2 + 2 * axis
                sh_ref[plus, rows, left] = (real_cos - imag_sin).astype(jnp.bfloat16)
                sh_ref[plus, rows, right] = (real_sin + imag_cos).astype(jnp.bfloat16)
                sh_ref[minus, rows, left] = (real_cos + imag_sin).astype(jnp.bfloat16)
                sh_ref[minus, rows, right] = (imag_cos - real_sin).astype(jnp.bfloat16)


def score_images(sh_ref, arrived, live, score_ref):
    scale = 2.0 / math.sqrt(arrived.shape[1])
    top = None
    for t in range(SHIFTS):
        score = scale * lax.dot_general(arrived, sh_ref[t], NT, preferred_element_type=jnp.float32)
        score = jnp.where(live > 0, score, NEGATIVE)
        score_ref[t] = score
        best = jnp.max(score, axis=0, keepdims=True)
        top = best if top is None else jnp.maximum(top, best)
    total = jnp.zeros_like(top)
    for t in range(SHIFTS):
        terms = jnp.where(live > 0, jnp.exp(score_ref[t] - top), 0.0)
        total = total + jnp.sum(terms, axis=0, keepdims=True)
    return top, total


def merge_stats(tops, totals):
    top = tops[0]
    for other in tops[1:]:
        top = jnp.maximum(top, other)
    total = sum(t * jnp.exp(m - top) for m, t in zip(tops, totals))
    return top + jnp.log(total)


def weigh(score_ref, live, evidence):
    return [
        jnp.where(live > 0, jnp.exp(score_ref[t] - evidence), 0.0).astype(jnp.bfloat16)
        for t in range(SHIFTS)
    ]


def low_table(ids):
    low = jnp.bitwise_and(ids, LOW - 1)
    hit = lax.broadcasted_iota(jnp.int32, (LOW, ids.shape[1]), 0) == low
    return jnp.where(hit, 1.0, 0.0).astype(jnp.bfloat16)


def insert_row(ids, table, real, imag):
    count = ids.shape[1]
    highs = VOX // LOW
    high = jnp.right_shift(ids, 7)
    hit = lax.broadcasted_iota(jnp.int32, (highs, count), 0) == high
    pieces = []
    for value in (real, imag):
        coarse = value.astype(jnp.bfloat16).astype(jnp.float32)
        for piece in (coarse, value - coarse):
            pieces.append(jnp.where(hit, piece, 0.0).astype(jnp.bfloat16))
    return lax.dot_general(
        jnp.concatenate(pieces, axis=0), table, NT, preferred_element_type=jnp.float32
    )


MESH = pl.DeviceIdType.MESH


def step_kernel(
    img_count,
    ref_count,
    sig_ref,
    part_ref,
    table_ref,
    proj_ref,
    ids_ref,
    volume_ref,
    evidence_ref,
    sh_ref,
    out_ref,
    slot_ref,
    arrived_ref,
    live_ref,
    score_ref,
    stat_ref,
    partial_ref,
    return_ref,
    far_ref,
    joint_ref,
    joined_ref,
    low_ref,
    block_send,
    block_recv,
    stat_send,
    stat_recv,
    sum_send,
    sum_recv,
    far_send,
    far_recv,
    join_send,
    join_recv,
):
    img = lax.axis_index("img")
    ref = lax.axis_index("ref")
    blocks, block_rows, features = proj_ref.shape
    pixels = features // 2
    chunks, _, _, span = partial_ref.shape
    half = span // 2
    particles = part_ref.shape[0]

    side = img_count // 2
    place = lax.rem(img, side)
    base = img - place
    mirror = lax.rem(img + side, img_count)

    def ahead(d):
        return lax.rem(base + (d // side) * side, img_count) + lax.rem(place + d % side, side)

    def behind(d):
        return lax.rem(base + (d // side) * side, img_count) + lax.rem(place - d % side + side, side)

    barrier = pltpu.get_barrier_semaphore()
    for d in range(1, img_count):
        pl.semaphore_signal(barrier, inc=1, device_id={"img": ahead(d)}, device_id_type=MESH)
    for d in range(1, ref_count):
        pl.semaphore_signal(
            barrier, inc=1, device_id={"ref": lax.rem(ref + d, ref_count)}, device_id_type=MESH
        )

    own = (img * ref_count + ref) * blocks

    def asked(d, k):
        return sig_ref[ahead(d), own + k]

    def asked_mirror(d, k):
        return sig_ref[ahead(d), (mirror * ref_count + ref) * blocks + k]

    for d in range(img_count):
        chosen = jnp.zeros((block_rows, features), jnp.float32)
        for k in range(blocks):
            chosen = jnp.where(asked(d, k) > 0, proj_ref[k].astype(jnp.float32), chosen)
        chosen = jnp.concatenate([chosen[:, :pixels], chosen[:, pixels:]], axis=0)
        out_ref[d] = chosen.astype(jnp.bfloat16)
    pl.semaphore_wait(barrier, img_count + ref_count - 2)

    block_copies = {}
    for d in range(1, img_count):
        block_copies[d] = pltpu.make_async_remote_copy(
            src_ref=out_ref.at[d],
            dst_ref=slot_ref.at[d],
            send_sem=block_send.at[d],
            recv_sem=block_recv.at[d],
            device_id={"img": ahead(d)},
            device_id_type=MESH,
        )
        block_copies[d].start()

    for d in range(img_count):
        alive = jnp.int32(0)
        source = behind(d)
        for k in range(blocks):
            alive = alive + sig_ref[img, (source * ref_count + ref) * blocks + k]
        live_ref[pl.ds(d * block_rows, block_rows), :] = jnp.full(
            (block_rows, particles), alive.astype(jnp.float32)
        )
    shift_images(part_ref, table_ref, sh_ref)
    held = low_ref.shape[2] == pixels
    for k in range(blocks if held else 0):
        for e in range(block_rows):
            for j in range(chunks):
                columns = pl.ds(j * half, half)
                low_ref[k * block_rows + e, :, columns] = low_table(ids_ref[k, e : e + 1, columns])

    slot_ref[0] = out_ref[0]
    for d in range(1, img_count):
        block_copies[d].wait_recv()
    for d in range(0, img_count, 2):
        pair = [slot_ref[d].astype(jnp.float32), slot_ref[d + 1].astype(jnp.float32)]
        for c in range(2):
            rows = jnp.concatenate([p[c * block_rows : (c + 1) * block_rows] for p in pair], axis=0)
            arrived_ref[pl.ds(d * block_rows, 2 * block_rows), pl.ds(c * pixels, pixels)] = rows.astype(
                jnp.bfloat16
            )

    live = live_ref[...]
    top, total = score_images(sh_ref, arrived_ref[...], live, score_ref)
    stat_ref[0] = jnp.zeros_like(stat_ref[0])
    stat_ref[0, 0:1, :] = top
    stat_ref[0, 1:2, :] = total
    stat_copies = []
    for d in range(1, ref_count):
        copy = pltpu.make_async_remote_copy(
            src_ref=stat_ref.at[0],
            dst_ref=stat_ref.at[d],
            send_sem=stat_send.at[d],
            recv_sem=stat_recv.at[d],
            device_id={"ref": lax.rem(ref + d, ref_count)},
            device_id_type=MESH,
        )
        copy.start()
        stat_copies.append(copy)
    for copy in stat_copies:
        copy.wait_recv()
    evidence = merge_stats(
        [stat_ref[r, 0:1, :] for r in range(ref_count)],
        [stat_ref[r, 1:2, :] for r in range(ref_count)],
    )
    evidence_ref[...] = evidence
    weights = weigh(score_ref, live, evidence)

    sum_copies = [[] for _ in range(chunks)]
    far_copies = [[] for _ in range(chunks)]
    join_copies = []

    def join(j):
        for copy in far_copies[j]:
            copy.wait_recv()
        for k in range(blocks):
            joint = jnp.where(asked_mirror(0, k) > 0, partial_ref[j, side], 0.0)
            for d in range(1, side):
                joint = joint + jnp.where(asked_mirror(d, k) > 0, far_ref[j, d], 0.0)
            joint_ref[j, k] = joint
        copy = pltpu.make_async_remote_copy(
            src_ref=joint_ref.at[j],
            dst_ref=joined_ref.at[j],
            send_sem=join_send.at[j],
            recv_sem=join_recv.at[j],
            device_id={"img": mirror},
            device_id_type=MESH,
        )
        copy.start()
        join_copies.append(copy)

    for j in range(chunks):
        for c in range(2):
            columns = pl.ds(c * pixels + j * half, half)
            partial = None
            for t in range(SHIFTS):
                term = lax.dot_general(
                    weights[t], sh_ref[t, :, columns], NN, preferred_element_type=jnp.float32
                )
                partial = term if partial is None else partial + term
            for d in range(img_count):
                rows = partial[d * block_rows : (d + 1) * block_rows]
                partial_ref[j, d, :, pl.ds(c * half, half)] = rows
        for d in range(1, side):
            copy = pltpu.make_async_remote_copy(
                src_ref=partial_ref.at[j, side + d],
                dst_ref=far_ref.at[j, d],
                send_sem=far_send.at[j, d],
                recv_sem=far_recv.at[j, d],
                device_id={"img": behind(d)},
                device_id_type=MESH,
            )
            copy.start()
            far_copies[j].append(copy)
        for d in range(1, side):
            copy = pltpu.make_async_remote_copy(
                src_ref=partial_ref.at[j, d],
                dst_ref=return_ref.at[j, d],
                send_sem=sum_send.at[j, d],
                recv_sem=sum_recv.at[j, d],
                device_id={"img": behind(d)},
                device_id_type=MESH,
            )
            copy.start()
            sum_copies[j].append(copy)
        if j > 0:
            join(j - 1)
    join(chunks - 1)

    highs = VOX // LOW
    slab = jnp.zeros((4 * highs, LOW), jnp.float32)
    for j in range(chunks):
        for copy in sum_copies[j]:
            copy.wait_recv()
        join_copies[j].wait_recv()
        for k in range(blocks):
            weighted = joined_ref[j, k] + jnp.where(asked(0, k) > 0, partial_ref[j, 0], 0.0)
            for d in range(1, side):
                weighted = weighted + jnp.where(asked(d, k) > 0, return_ref[j, d], 0.0)
            for e in range(block_rows):
                ids = ids_ref[k, e : e + 1, pl.ds(j * half, half)]
                slab = slab + insert_row(
                    ids,
                    low_ref[k * block_rows + e, :, pl.ds(j * half, half)] if held else low_table(ids),
                    weighted[e : e + 1, :half],
                    weighted[e : e + 1, half:],
                )
    for c in range(2):
        part = slab[2 * c * highs : (2 * c + 1) * highs]
        part = part + slab[(2 * c + 1) * highs : (2 * c + 2) * highs]
        for h in range(highs):
            volume_ref[c : c + 1, h * LOW : (h + 1) * LOW] = part[h : h + 1]

    for d in range(1, img_count):
        block_copies[d].wait_send()
    for copy in stat_copies:
        copy.wait_send()
    for copies in sum_copies + far_copies + [join_copies]:
        for copy in copies:
            copy.wait_send()


VMEM = pl.BlockSpec(memory_space=pltpu.VMEM)
SMEM = pl.BlockSpec(memory_space=pltpu.SMEM)
CHUNKS = 4


def per_device(particles, projections, significance, insertion):
    img_count = lax.axis_size("img")
    ref_count = lax.axis_size("ref")
    blocks_here, block_rows, features = projections.shape
    particle_count = particles.shape[0]
    width = img_count * block_rows
    pixels = features // 2
    table = jnp.asarray(rotation_tables(pixels))
    volume, evidence = pl.pallas_call(
        functools.partial(step_kernel, img_count, ref_count),
        out_shape=(
            jax.ShapeDtypeStruct((2, VOX), jnp.float32),
            jax.ShapeDtypeStruct((1, particle_count), jnp.float32),
        ),
        in_specs=[SMEM] + [VMEM] * 4,
        out_specs=(VMEM,) * 2,
        scratch_shapes=[
            pltpu.VMEM((SHIFTS, particle_count, features), jnp.bfloat16),
            pltpu.VMEM((img_count, 2 * block_rows, pixels), jnp.bfloat16),
            pltpu.VMEM((img_count, 2 * block_rows, pixels), jnp.bfloat16),
            pltpu.VMEM((width, features), jnp.bfloat16),
            pltpu.VMEM((width, particle_count), jnp.float32),
            pltpu.VMEM((SHIFTS, width, particle_count), jnp.float32),
            pltpu.VMEM((ref_count, 8, particle_count), jnp.float32),
            pltpu.VMEM((CHUNKS, img_count, block_rows, features // CHUNKS), jnp.float32),
            pltpu.VMEM((CHUNKS, img_count // 2, block_rows, features // CHUNKS), jnp.float32),
            pltpu.VMEM((CHUNKS, img_count // 2, block_rows, features // CHUNKS), jnp.float32),
            pltpu.VMEM((CHUNKS, blocks_here, block_rows, features // CHUNKS), jnp.float32),
            pltpu.VMEM((CHUNKS, blocks_here, block_rows, features // CHUNKS), jnp.float32),
            pltpu.VMEM((blocks_here * block_rows, LOW, pixels if width <= 128 else LOW), jnp.bfloat16),
            pltpu.SemaphoreType.DMA((img_count,)),
            pltpu.SemaphoreType.DMA((img_count,)),
            pltpu.SemaphoreType.DMA((ref_count,)),
            pltpu.SemaphoreType.DMA((ref_count,)),
            pltpu.SemaphoreType.DMA((CHUNKS, img_count // 2)),
            pltpu.SemaphoreType.DMA((CHUNKS, img_count // 2)),
            pltpu.SemaphoreType.DMA((CHUNKS, img_count // 2)),
            pltpu.SemaphoreType.DMA((CHUNKS, img_count // 2)),
            pltpu.SemaphoreType.DMA((CHUNKS,)),
            pltpu.SemaphoreType.DMA((CHUNKS,)),
        ],
        compiler_params=pltpu.CompilerParams(
            vmem_limit_bytes=VMEM_BYTES, collective_id=0, has_side_effects=True
        ),
    )(significance, particles, table, projections, insertion)
    return volume, evidence.reshape(particle_count)


def solution(mesh):
    in_specs = (P("img", None), P(("img", "ref"), None, None), P(), P(("img", "ref"), None, None))
    out_specs = (P(None, ("img", "ref")), P("img"))
    return jax.shard_map(
        per_device, mesh=mesh, in_specs=in_specs, out_specs=out_specs, check_vma=False
    )
```

```python
import functools
import math

import jax
import jax.numpy as jnp
import numpy as np
from jax import lax
from jax.experimental import pallas as pl
from jax.experimental.pallas import tpu as pltpu
from jax.sharding import PartitionSpec as P

SIDE = 64
VOX = 4096
LOW = 128
SHIFTS = 5
NEGATIVE = -1e30
ROWS = 16
COLS = 512
VMEM_BYTES = 56 * 1024 * 1024
NT = (((1,), (1,)), ((), ()))
NN = (((1,), (0,)), ((), ()))


def rotation_tables(pixels):
    positions = np.arange(pixels, dtype=np.int64)
    step = np.float32(2.0 * math.pi / SIDE)
    angle_x = (step * (positions % SIDE - SIDE // 2).astype(np.float32)).astype(np.float64)
    angle_y = (step * (positions // SIDE).astype(np.float32)).astype(np.float64)
    table = np.stack([np.cos(angle_x), np.sin(angle_x), np.cos(angle_y), np.sin(angle_y)])
    return np.concatenate([table, np.zeros_like(table)]).astype(np.float32)


def shift_images(part_ref, table_ref, sh_ref, first, last):
    pixels = part_ref.shape[1] // 2

    @pl.loop(first // ROWS, last // ROWS)
    def _(step):
        rows = pl.ds(pl.multiple_of(step * ROWS, ROWS), ROWS)
        for start in range(0, pixels, COLS):
            left = pl.ds(start, COLS)
            right = pl.ds(pixels + start, COLS)
            real16 = part_ref[rows, left]
            imag16 = part_ref[rows, right]
            sh_ref[0, rows, left] = real16
            sh_ref[0, rows, right] = imag16
            real = real16.astype(jnp.float32)
            imag = imag16.astype(jnp.float32)
            for axis in range(2):
                cosine = table_ref[2 * axis : 2 * axis + 1, left]
                sine = table_ref[2 * axis + 1 : 2 * axis + 2, left]
                real_cos, imag_sin = real * cosine, imag * sine
                real_sin, imag_cos = real * sine, imag * cosine
                plus, minus = 1 + 2 * axis, 2 + 2 * axis
                sh_ref[plus, rows, left] = (real_cos - imag_sin).astype(jnp.bfloat16)
                sh_ref[plus, rows, right] = (real_sin + imag_cos).astype(jnp.bfloat16)
                sh_ref[minus, rows, left] = (real_cos + imag_sin).astype(jnp.bfloat16)
                sh_ref[minus, rows, right] = (imag_cos - real_sin).astype(jnp.bfloat16)


def score_images(sh_ref, arrived, live, score_ref):
    scale = 2.0 / math.sqrt(arrived.shape[1])
    top = None
    for t in range(SHIFTS):
        score = scale * lax.dot_general(arrived, sh_ref[t], NT, preferred_element_type=jnp.float32)
        score = jnp.where(live > 0, score, NEGATIVE)
        score_ref[t] = score
        best = jnp.max(score, axis=0, keepdims=True)
        top = best if top is None else jnp.maximum(top, best)
    total = jnp.zeros_like(top)
    for t in range(SHIFTS):
        terms = jnp.where(live > 0, jnp.exp(score_ref[t] - top), 0.0)
        total = total + jnp.sum(terms, axis=0, keepdims=True)
    return top, total


def merge_stats(tops, totals):
    top = tops[0]
    for other in tops[1:]:
        top = jnp.maximum(top, other)
    total = sum(t * jnp.exp(m - top) for m, t in zip(tops, totals))
    return top + jnp.log(total)


def weigh(score_ref, live, evidence):
    return [
        jnp.where(live > 0, jnp.exp(score_ref[t] - evidence), 0.0).astype(jnp.bfloat16)
        for t in range(SHIFTS)
    ]


def low_table(ids):
    low = jnp.bitwise_and(ids, LOW - 1)
    hit = lax.broadcasted_iota(jnp.int32, (LOW, ids.shape[1]), 0) == low
    return jnp.where(hit, 1.0, 0.0).astype(jnp.bfloat16)


def insert_row(ids, table, real, imag):
    count = ids.shape[1]
    highs = VOX // LOW
    high = jnp.right_shift(ids, 7)
    hit = lax.broadcasted_iota(jnp.int32, (highs, count), 0) == high
    pieces = []
    for value in (real, imag):
        coarse = value.astype(jnp.bfloat16).astype(jnp.float32)
        for piece in (coarse, value - coarse):
            pieces.append(jnp.where(hit, piece, 0.0).astype(jnp.bfloat16))
    return lax.dot_general(
        jnp.concatenate(pieces, axis=0), table, NT, preferred_element_type=jnp.float32
    )


MESH = pl.DeviceIdType.MESH


def step_kernel(
    img_count,
    ref_count,
    sig_ref,
    part_ref,
    table_ref,
    proj_ref,
    ids_ref,
    volume_ref,
    evidence_ref,
    sh_ref,
    out_ref,
    slot_ref,
    arrived_ref,
    live_ref,
    score_ref,
    stat_ref,
    partial_ref,
    return_ref,
    far_ref,
    joint_ref,
    joined_ref,
    low_ref,
    pack_ref,
    pair_ref,
    block_send,
    block_recv,
    stat_send,
    stat_recv,
    sum_send,
    sum_recv,
    far_send,
    far_recv,
    join_send,
    join_recv,
):
    img = lax.axis_index("img")
    ref = lax.axis_index("ref")
    blocks, block_rows, features = proj_ref.shape
    pixels = features // 2
    chunks, _, _, span = partial_ref.shape
    half = span // 2
    particles = part_ref.shape[0]

    side = img_count // 2
    place = lax.rem(img, side)
    base = img - place
    mirror = lax.rem(img + side, img_count)

    def ahead(d):
        return lax.rem(base + (d // side) * side, img_count) + lax.rem(place + d % side, side)

    def behind(d):
        return lax.rem(base + (d // side) * side, img_count) + lax.rem(place - d % side + side, side)

    barrier = pltpu.get_barrier_semaphore()
    for d in range(1, img_count):
        pl.semaphore_signal(barrier, inc=1, device_id={"img": ahead(d)}, device_id_type=MESH)
    for d in range(1, ref_count):
        pl.semaphore_signal(
            barrier, inc=1, device_id={"ref": lax.rem(ref + d, ref_count)}, device_id_type=MESH
        )

    own = (img * ref_count + ref) * blocks

    def asked(d, k):
        return sig_ref[ahead(d), own + k]

    def asked_mirror(d, k):
        return sig_ref[ahead(d), (mirror * ref_count + ref) * blocks + k]

    for k in range(blocks):
        whole = proj_ref[k].astype(jnp.float32)
        whole = jnp.concatenate([whole[:, :pixels], whole[:, pixels:]], axis=0)
        pack_ref[k] = whole.astype(jnp.bfloat16)

    def choose(d, source_ref, wanted):
        chosen = jnp.zeros(source_ref.shape[1:], jnp.float32)
        for k in range(blocks):
            chosen = jnp.where(wanted(d, k) > 0, source_ref[k].astype(jnp.float32), chosen)
        return chosen.astype(jnp.bfloat16)

    for d in range(1, side):
        out_ref[d] = choose(d, pack_ref, asked)
    pl.semaphore_wait(barrier, img_count + ref_count - 2)

    block_copies = {}

    def send_block(d, source, target, device):
        block_copies[d] = pltpu.make_async_remote_copy(
            src_ref=source,
            dst_ref=target,
            send_sem=block_send.at[d],
            recv_sem=block_recv.at[d],
            device_id={"img": device},
            device_id_type=MESH,
        )
        block_copies[d].start()

    send_block(side, pack_ref, pair_ref, mirror)
    for d in range(1, side):
        send_block(d, out_ref.at[d], slot_ref.at[d], ahead(d))

    for d in range(img_count):
        alive = jnp.int32(0)
        source = behind(d)
        for k in range(blocks):
            alive = alive + sig_ref[img, (source * ref_count + ref) * blocks + k]
        live_ref[pl.ds(d * block_rows, block_rows), :] = jnp.full(
            (block_rows, particles), alive.astype(jnp.float32)
        )
    slot_ref[0] = choose(0, pack_ref, asked)
    shift_images(part_ref, table_ref, sh_ref, 0, particles // 2)
    block_copies[side].wait_recv()
    for d in range(1, side):
        out_ref[side + d] = choose(d, pair_ref, asked_mirror)
        send_block(side + d, out_ref.at[side + d], slot_ref.at[side + d], ahead(d))
    slot_ref[side] = choose(0, pair_ref, asked_mirror)
    shift_images(part_ref, table_ref, sh_ref, particles // 2, particles)
    held = low_ref.shape[2] == pixels
    for k in range(blocks if held else 0):
        for e in range(block_rows):
            for j in range(chunks):
                columns = pl.ds(j * half, half)
                low_ref[k * block_rows + e, :, columns] = low_table(ids_ref[k, e : e + 1, columns])

    for d in range(1, img_count):
        if d != side:
            block_copies[d].wait_recv()
    for d in range(0, img_count, 2):
        pair = [slot_ref[d].astype(jnp.float32), slot_ref[d + 1].astype(jnp.float32)]
        for c in range(2):
            rows = jnp.concatenate([p[c * block_rows : (c + 1) * block_rows] for p in pair], axis=0)
            arrived_ref[pl.ds(d * block_rows, 2 * block_rows), pl.ds(c * pixels, pixels)] = rows.astype(
                jnp.bfloat16
            )

    live = live_ref[...]
    top, total = score_images(sh_ref, arrived_ref[...], live, score_ref)
    stat_ref[0] = jnp.zeros_like(stat_ref[0])
    stat_ref[0, 0:1, :] = top
    stat_ref[0, 1:2, :] = total
    stat_copies = []
    for d in range(1, ref_count):
        copy = pltpu.make_async_remote_copy(
            src_ref=stat_ref.at[0],
            dst_ref=stat_ref.at[d],
            send_sem=stat_send.at[d],
            recv_sem=stat_recv.at[d],
            device_id={"ref": lax.rem(ref + d, ref_count)},
            device_id_type=MESH,
        )
        copy.start()
        stat_copies.append(copy)
    for copy in stat_copies:
        copy.wait_recv()
    evidence = merge_stats(
        [stat_ref[r, 0:1, :] for r in range(ref_count)],
        [stat_ref[r, 1:2, :] for r in range(ref_count)],
    )
    evidence_ref[...] = evidence
    weights = weigh(score_ref, live, evidence)

    sum_copies = [[] for _ in range(chunks)]
    far_copies = [[] for _ in range(chunks)]
    join_copies = []

    def join(j):
        for copy in far_copies[j]:
            copy.wait_recv()
        for k in range(blocks):
            joint = jnp.where(asked_mirror(0, k) > 0, partial_ref[j, side], 0.0)
            for d in range(1, side):
                joint = joint + jnp.where(asked_mirror(d, k) > 0, far_ref[j, d], 0.0)
            joint_ref[j, k] = joint
        copy = pltpu.make_async_remote_copy(
            src_ref=joint_ref.at[j],
            dst_ref=joined_ref.at[j],
            send_sem=join_send.at[j],
            recv_sem=join_recv.at[j],
            device_id={"img": mirror},
            device_id_type=MESH,
        )
        copy.start()
        join_copies.append(copy)

    for j in range(chunks):
        for c in range(2):
            columns = pl.ds(c * pixels + j * half, half)
            partial = None
            for t in range(SHIFTS):
                term = lax.dot_general(
                    weights[t], sh_ref[t, :, columns], NN, preferred_element_type=jnp.float32
                )
                partial = term if partial is None else partial + term
            for d in range(img_count):
                rows = partial[d * block_rows : (d + 1) * block_rows]
                partial_ref[j, d, :, pl.ds(c * half, half)] = rows
        for d in range(1, side):
            copy = pltpu.make_async_remote_copy(
                src_ref=partial_ref.at[j, side + d],
                dst_ref=far_ref.at[j, d],
                send_sem=far_send.at[j, d],
                recv_sem=far_recv.at[j, d],
                device_id={"img": behind(d)},
                device_id_type=MESH,
            )
            copy.start()
            far_copies[j].append(copy)
        for d in range(1, side):
            copy = pltpu.make_async_remote_copy(
                src_ref=partial_ref.at[j, d],
                dst_ref=return_ref.at[j, d],
                send_sem=sum_send.at[j, d],
                recv_sem=sum_recv.at[j, d],
                device_id={"img": behind(d)},
                device_id_type=MESH,
            )
            copy.start()
            sum_copies[j].append(copy)
        if j > 0:
            join(j - 1)
    join(chunks - 1)

    highs = VOX // LOW
    slab = jnp.zeros((4 * highs, LOW), jnp.float32)
    for j in range(chunks):
        for copy in sum_copies[j]:
            copy.wait_recv()
        join_copies[j].wait_recv()
        for k in range(blocks):
            weighted = joined_ref[j, k] + jnp.where(asked(0, k) > 0, partial_ref[j, 0], 0.0)
            for d in range(1, side):
                weighted = weighted + jnp.where(asked(d, k) > 0, return_ref[j, d], 0.0)
            for e in range(block_rows):
                ids = ids_ref[k, e : e + 1, pl.ds(j * half, half)]
                slab = slab + insert_row(
                    ids,
                    low_ref[k * block_rows + e, :, pl.ds(j * half, half)] if held else low_table(ids),
                    weighted[e : e + 1, :half],
                    weighted[e : e + 1, half:],
                )
    for c in range(2):
        part = slab[2 * c * highs : (2 * c + 1) * highs]
        part = part + slab[(2 * c + 1) * highs : (2 * c + 2) * highs]
        for h in range(highs):
            volume_ref[c : c + 1, h * LOW : (h + 1) * LOW] = part[h : h + 1]

    for d in range(1, img_count):
        block_copies[d].wait_send()
    for copy in stat_copies:
        copy.wait_send()
    for copies in sum_copies + far_copies + [join_copies]:
        for copy in copies:
            copy.wait_send()


VMEM = pl.BlockSpec(memory_space=pltpu.VMEM)
SMEM = pl.BlockSpec(memory_space=pltpu.SMEM)
CHUNKS = 4


def per_device(particles, projections, significance, insertion):
    img_count = lax.axis_size("img")
    ref_count = lax.axis_size("ref")
    blocks_here, block_rows, features = projections.shape
    particle_count = particles.shape[0]
    width = img_count * block_rows
    pixels = features // 2
    table = jnp.asarray(rotation_tables(pixels))
    volume, evidence = pl.pallas_call(
        functools.partial(step_kernel, img_count, ref_count),
        out_shape=(
            jax.ShapeDtypeStruct((2, VOX), jnp.float32),
            jax.ShapeDtypeStruct((1, particle_count), jnp.float32),
        ),
        in_specs=[SMEM] + [VMEM] * 4,
        out_specs=(VMEM,) * 2,
        scratch_shapes=[
            pltpu.VMEM((SHIFTS, particle_count, features), jnp.bfloat16),
            pltpu.VMEM((img_count, 2 * block_rows, pixels), jnp.bfloat16),
            pltpu.VMEM((img_count, 2 * block_rows, pixels), jnp.bfloat16),
            pltpu.VMEM((width, features), jnp.bfloat16),
            pltpu.VMEM((width, particle_count), jnp.float32),
            pltpu.VMEM((SHIFTS, width, particle_count), jnp.float32),
            pltpu.VMEM((ref_count, 8, particle_count), jnp.float32),
            pltpu.VMEM((CHUNKS, img_count, block_rows, features // CHUNKS), jnp.float32),
            pltpu.VMEM((CHUNKS, img_count // 2, block_rows, features // CHUNKS), jnp.float32),
            pltpu.VMEM((CHUNKS, img_count // 2, block_rows, features // CHUNKS), jnp.float32),
            pltpu.VMEM((CHUNKS, blocks_here, block_rows, features // CHUNKS), jnp.float32),
            pltpu.VMEM((CHUNKS, blocks_here, block_rows, features // CHUNKS), jnp.float32),
            pltpu.VMEM((blocks_here * block_rows, LOW, pixels if width <= 128 else LOW), jnp.bfloat16),
            pltpu.VMEM((blocks_here, 2 * block_rows, pixels), jnp.bfloat16),
            pltpu.VMEM((blocks_here, 2 * block_rows, pixels), jnp.bfloat16),
            pltpu.SemaphoreType.DMA((img_count,)),
            pltpu.SemaphoreType.DMA((img_count,)),
            pltpu.SemaphoreType.DMA((ref_count,)),
            pltpu.SemaphoreType.DMA((ref_count,)),
            pltpu.SemaphoreType.DMA((CHUNKS, img_count // 2)),
            pltpu.SemaphoreType.DMA((CHUNKS, img_count // 2)),
            pltpu.SemaphoreType.DMA((CHUNKS, img_count // 2)),
            pltpu.SemaphoreType.DMA((CHUNKS, img_count // 2)),
            pltpu.SemaphoreType.DMA((CHUNKS,)),
            pltpu.SemaphoreType.DMA((CHUNKS,)),
        ],
        compiler_params=pltpu.CompilerParams(
            vmem_limit_bytes=VMEM_BYTES, collective_id=0, has_side_effects=True
        ),
    )(significance, particles, table, projections, insertion)
    return volume, evidence.reshape(particle_count)


def solution(mesh):
    in_specs = (P("img", None), P(("img", "ref"), None, None), P(), P(("img", "ref"), None, None))
    out_specs = (P(None, ("img", "ref")), P("img"))
    return jax.shard_map(
        per_device, mesh=mesh, in_specs=in_specs, out_specs=out_specs, check_vma=False
    )
```
